512 devices in a mesh: dp: 8 (over x, core), mp: 64 (over z, y).
Axes of the slice: x: 4, y: 8, z: 8, core: 2. Of those that a mesh axis runs over, the one named last changes fastest.
Arguments:
- grad_parts: bfloat16 [8, 64, 4, 512, 512], P('dp', 'mp'), may hold values from -0.09375 to 0.09375
- factors: float32 [64, 8, 512, 512], P('mp', 'dp'), may hold values from -1 to 8, as said below
- root_prev: bfloat16 [64, 8, 512, 512], P(None, 'dp', 'mp'), may hold values from -1 to 2, as said below
- plan: int32 [8, 64], P('dp'), may hold values from 0 to 64, as said below
Outputs:
- new_factors: float32 [64, 8, 512, 512], P('mp', 'dp')
- new_roots: bfloat16 [64, 8, 512, 512], P(None, 'dp', 'mp')
The draws below stay inside these ranges and needn't reach their ends.
Inputs may be any that keep to these rules, and one draw needn't show every extreme that they name: In each row of plan no worker is named more than 3 times and one is named exactly 3 times; at least 32 entries of a row are below 64. `factors`: each factor is symmetric. `root_prev`: each root is symmetric.
All inputs are finite; a program needn't handle non-finite values.
Results may differ from the reference program's by a relative error of at most 0.0055.
Values may be sent and summed in bfloat16 or wider, within the bound.
No kernel may reach another device: no remote copies, remote signals or barrier semaphores. Data moves between devices by JAX's collectives and lax.ppermute only.
A program may use at most 64 MiB of HBM per device.

```python
import jax
import jax.numpy as jnp
from jax import lax

BS = 512
CAP = 3
HALF = 4
N_DP = 8
N_MP = 64


def spectrum(key):
    upper_end = 4.0
    uniform_draw = jax.random.uniform(jax.random.fold_in(key, 11), (N_MP, N_DP, BS), jnp.float32)
    return 0.5 * jnp.exp(uniform_draw * jnp.log(upper_end / 0.5))


def symmetric(key):
    noise = jax.random.normal(key, (N_MP, N_DP, BS, BS), jnp.float32)
    return (noise + jnp.swapaxes(noise, -1, -2)) * 0.5 ** 0.5


def draw_factors(key, part):
    diagonal_vals = spectrum(key)
    identity = jnp.eye(BS, dtype=jnp.float32)
    outer_scale = jnp.sqrt(diagonal_vals[..., :, None] * diagonal_vals[..., None, :])
    spread = symmetric(jax.random.fold_in(key, 12)) * (0.25 / BS ** 0.5)
    result = outer_scale * spread * (1.0 - identity) + identity * diagonal_vals[..., None, :]
    return result.astype(jnp.float32)


def draw_root_prev(key, part):
    diagonal_vals = spectrum(key)
    identity = jnp.eye(BS, dtype=jnp.float32)
    scaling = diagonal_vals ** (-0.125)
    spread = symmetric(jax.random.fold_in(key, 13)) * (0.2 / BS ** 0.5)
    inner = identity + spread * (1.0 - identity)
    result = scaling[..., :, None] * inner * scaling[..., None, :]
    return result.astype(jnp.bfloat16)


def plan_row(key):
    refreshed = jax.random.randint(jax.random.fold_in(key, 1), (), N_MP // 2, N_MP + 1)
    rank_of = jax.random.permutation(jax.random.fold_in(key, 2), N_MP)
    shuffled = jax.random.permutation(jax.random.fold_in(key, 3), N_MP)
    busiest = shuffled[0]
    remaining = shuffled[1:]
    workers = jnp.concatenate([jnp.full((CAP,), busiest), jnp.full((2,), remaining[0]), remaining[1:]])
    chosen = workers[rank_of]
    return jnp.where(rank_of < refreshed, chosen, N_MP).astype(jnp.int32)


def draw_plan(key, part):
    row_keys = jax.random.split(key, N_DP)
    return jax.vmap(plan_row)(row_keys)


def shard_levels(rng, extent, pieces, smallest, largest):
    level, own = 1.0, jax.random.fold_in(rng, 6)
    for axis_at, shards_of in pieces:
        heights = jnp.exp(jax.random.uniform(jax.random.fold_in(own, axis_at), (shards_of,), jnp.float32, smallest / len(pieces), largest / len(pieces)))
        level = level * jnp.repeat(heights, extent[axis_at] // shards_of).reshape([-1 if axis == axis_at else 1 for axis in range(len(extent))])
    return level


def normal_values(rng, dims, deviation, bound, pieces=(), kind=jnp.bfloat16):
    level = shard_levels(rng, dims, pieces, -0.22, 0.18) if pieces else 1.0
    values = jax.random.normal(rng, dims, jnp.float32) * deviation * level
    return jnp.minimum(jnp.maximum(values, -bound), bound).astype(kind)


def setup_inputs(seed: int = 0) -> dict:
    streams_of = jax.random.split(jax.random.key(seed), 5)
    grad_parts = normal_values(streams_of[0], (N_DP, N_MP, HALF, BS, BS), (BS * N_DP) ** -0.5, 0.09375, ((0, 8), (1, 64)))
    factors = draw_factors(jax.random.fold_in(streams_of[4], 71), 0)
    root_prev = draw_root_prev(jax.random.fold_in(streams_of[4], 71), 0)
    plan = draw_plan(jax.random.fold_in(streams_of[4], 71), 0)
    return dict(grad_parts=grad_parts, factors=factors, root_prev=root_prev, plan=plan)


keep_rate = 0.8


def newton(initial, factor):
    identity = jnp.eye(factor.shape[-1], dtype=jnp.float32)
    square = jnp.einsum("sij,sjk->sik", initial, initial, preferred_element_type=jnp.float32)
    fourth = jnp.einsum("sij,sjk->sik", square, square, precision=lax.Precision.HIGHEST)
    coupled = jnp.einsum("sij,sjk->sik", fourth, factor, precision=lax.Precision.HIGHEST)
    update = (5.0 * identity - coupled) * 0.25
    return jnp.einsum("sij,sjk->sik", initial.astype(jnp.float32), update, precision=lax.Precision.HIGHEST)


def reference(grad_parts, factors, root_prev, plan):
    def per_owner(owner):
        partial_grads = lax.dynamic_index_in_dim(grad_parts, owner, 1, keepdims=False)
        summed = jnp.sum(partial_grads.astype(jnp.float32), axis=0)
        left = jnp.einsum("kij,klj->kil", summed, summed, precision=lax.Precision.HIGHEST)
        right = jnp.einsum("kji,kjl->kil", summed, summed, precision=lax.Precision.HIGHEST)
        grams = jnp.stack([left, right], axis=1).reshape(N_DP, BS, BS)
        old_factor = lax.dynamic_index_in_dim(factors, owner, 0, keepdims=False)
        fresh_factor = keep_rate * old_factor + (1.0 - keep_rate) * grams
        previous = lax.dynamic_index_in_dim(root_prev, owner, 0, keepdims=False)
        refined = newton(previous, fresh_factor).astype(jnp.bfloat16)
        owner_plan = lax.dynamic_index_in_dim(plan, owner, 1, keepdims=False)
        roots = jnp.where(owner_plan[:, None, None] < N_MP, refined, previous)
        return fresh_factor, roots

    new_factors, new_roots = lax.map(per_owner, jnp.arange(N_MP, dtype=jnp.int32))
    return new_factors, new_roots
```

```python
import jax
import jax.numpy as jnp
from jax import lax
from jax.sharding import PartitionSpec as P

keep_rate = 0.8


def in_blocks(value, dim, length):
    before, after = (value.shape[:dim], value.shape[dim + 1 :])
    return jnp.moveaxis(value.reshape(*before, length, -1, *after), dim, 0)


def sum_at_owner(value, axis, dim):
    length = lax.axis_size(axis)
    pieces = lax.all_to_all(in_blocks(value, dim, length), axis, 0, 0, tiled=True)
    return jnp.sum(pieces.astype(jnp.float32), axis=0)


def swapped(value, axis, bit):
    return lax.ppermute(value, axis, [(i, i ^ 1 << bit) for i in range(lax.axis_size(axis))])


def newton(initial, factor):
    identity = jnp.eye(factor.shape[-1], dtype=jnp.float32)
    square = jnp.einsum("sij,sjk->sik", initial, initial, preferred_element_type=jnp.float32)
    fourth = jnp.einsum("sij,sjk->sik", square, square, precision=lax.Precision.HIGHEST)
    coupled = jnp.einsum("sij,sjk->sik", fourth, factor, precision=lax.Precision.HIGHEST)
    update = (5.0 * identity - coupled) * 0.25
    return jnp.einsum(
        "sij,sjk->sik", initial.astype(jnp.float32), update, precision=lax.Precision.HIGHEST
    )


def to_pieces(matrix):
    return lax.all_to_all(matrix, "mp", split_axis=0, concat_axis=0, tiled=True)


def local(grad_parts, factors, root_prev, plan):
    workers = lax.axis_size("mp")
    block_size = factors.shape[-1]
    rows = block_size // workers
    partial_grads = grad_parts.astype(jnp.float32).reshape(
        2 * grad_parts.shape[2], block_size // 2, block_size
    )
    my_half = sum_at_owner(partial_grads.astype(jnp.bfloat16), "dp", 0)[0]
    partner_half = swapped(my_half.astype(jnp.bfloat16), "dp", 0).astype(my_half.dtype)
    my_side = lax.axis_index("dp") % 2
    upper_rows = jnp.where(my_side == 0, my_half, partner_half)
    lower_rows = jnp.where(my_side == 0, partner_half, my_half)
    full_block = jnp.concatenate([upper_rows, lower_rows], axis=0)
    leading = jnp.where(my_side == 0, full_block, full_block.T)
    gram_new = jnp.dot(leading, leading.T, precision=lax.Precision.HIGHEST)
    fresh_factor = keep_rate * factors[0, 0] + (1.0 - keep_rate) * gram_new
    plan_row = plan[0]
    refresh = plan_row < workers
    old_pieces = root_prev.reshape(workers, rows, block_size)
    gathered = lax.all_to_all(old_pieces, "mp", split_axis=0, concat_axis=0, tiled=True)
    initial = gathered.reshape(1, block_size, block_size)
    own_entry = lax.dynamic_index_in_dim(plan_row, lax.axis_index("mp"), 0, keepdims=False)

    def refine_own():
        return newton(initial, fresh_factor[None])[0].astype(jnp.bfloat16)

    def keep_own():
        return initial[0]

    refined = lax.cond(own_entry < workers, refine_own, keep_own)
    fresh_roots = to_pieces(refined.reshape(workers, rows, block_size))
    new_roots = jnp.where(refresh[:, None, None], fresh_roots, old_pieces).reshape(root_prev.shape)
    return (fresh_factor[None, None], new_roots)


def solution(mesh):
    return jax.shard_map(
        local,
        mesh=mesh,
        in_specs=(
            P("dp", "mp", None, None, None),
            P("mp", "dp", None, None),
            P(None, "dp", "mp", None),
            P("dp", None),
        ),
        out_specs=(P("mp", "dp", None, None), P(None, "dp", "mp", None)),
        check_vma=False,
    )
```

```python
import jax
import jax.numpy as jnp
from jax import lax
from jax.experimental import pallas as pl
from jax.experimental.pallas import tpu as pltpu
from jax.sharding import PartitionSpec as P

keep_rate = 0.8
VMEM = pl.BlockSpec(memory_space=pltpu.VMEM)
ANY = pl.BlockSpec(memory_space=pl.ANY)
SMEM = pl.BlockSpec(memory_space=pltpu.SMEM)
PARAMS = pltpu.CompilerParams(vmem_limit_bytes=20 * 1024 * 1024)


def dot(a, b):
    return jnp.dot(a, b, preferred_element_type=jnp.float32)


def split(value):
    high = value.astype(jnp.bfloat16)
    return high, (value - high.astype(jnp.float32)).astype(jnp.bfloat16)


def fifth_kernel(root_ref, high_ref, low_ref):
    root = root_ref[...]
    high, low = split(dot(root, root))
    high, low = split(dot(high, high) + (dot(high, low) + dot(low, high)))
    high_ref[...], low_ref[...] = split(dot(root, high) + dot(root, low))


def prepare_kernel(x_ref, blocks_ref, plus_ref, minus_ref, sems):
    ring, size, _ = blocks_ref.shape
    half = size // 2
    x = x_ref[0]
    wanted = ((2, 0, plus_ref, 0), (1, half, plus_ref, 1), (2, half, minus_ref, 0), (3, 0, minus_ref, 1))
    copies = []
    for at, (step, row, target, slot) in enumerate(wanted):
        source = blocks_ref.at[lax.rem(x + step, ring), pl.ds(row, half)]
        copies.append(pltpu.make_async_copy(source, target.at[slot], sems.at[at]))
    for copy in copies:
        copy.start()
    for copy in copies:
        copy.wait()


def add(*values):
    return sum(value.astype(jnp.float32) for value in values).astype(jnp.bfloat16)


def relay_kernel(x_ref, right_ref, left_ref, from_left_ref, from_right_ref, upper_ref, lower_ref):
    upper_ref[...] = add(right_ref[0], from_left_ref[...])
    lower_ref[...] = add(left_ref[0], from_right_ref[...])


def finish_kernel(x_ref, own_ref, from_left_ref, from_right_ref, upper_ref, lower_ref, mine_ref):
    half = upper_ref.shape[0]
    mine_ref[:half] = add(own_ref[0, :half], from_right_ref[...], upper_ref[...])
    mine_ref[half:] = add(own_ref[0, half:], from_left_ref[...], lower_ref[...])


def refresh_kernel(side_ref, mine_ref, other_ref, factor_ref, root_ref, high_ref, low_ref, fresh_ref, refined_ref):
    summed = add(mine_ref[...], other_ref[...])

    def update(gram):
        fresh_ref[...] = keep_rate * factor_ref[...] + (1.0 - keep_rate) * gram

    @pl.when(side_ref[0] == 0)
    def _():
        update(lax.dot_general(summed, summed, (((1,), (1,)), ((), ())), preferred_element_type=jnp.float32))

    @pl.when(side_ref[0] != 0)
    def _():
        update(lax.dot_general(summed, summed, (((0,), (0,)), ((), ())), preferred_element_type=jnp.float32))

    high, low = split(fresh_ref[...])
    coupled = dot(high_ref[...], high) + (dot(high_ref[...], low) + dot(low_ref[...], high))
    refined_ref[...] = (1.25 * root_ref[...].astype(jnp.float32) - 0.25 * coupled).astype(jnp.bfloat16)


def cost(flops, moved):
    return pl.CostEstimate(flops=flops, bytes_accessed=moved, transcendentals=0)


def local(grad_parts, factors, root_prev, plan):
    workers = lax.axis_size("mp")
    replicas = lax.axis_size("dp")
    size = factors.shape[-1]
    half = size // 2
    blocks = grad_parts[0, 0]
    ring = blocks.shape[0]
    dp = lax.axis_index("dp")
    x, side = dp // 2, dp % 2

    def shifted(value, step):
        return lax.ppermute(value, "dp", [(i, (i // 2 + step) % ring * 2 + i % 2) for i in range(replicas)])

    pair = jax.ShapeDtypeStruct((2, half, size), jnp.bfloat16)
    part = jax.ShapeDtypeStruct((half, size), jnp.bfloat16)
    matrix = jax.ShapeDtypeStruct((size, size), jnp.bfloat16)
    place = x.reshape(1)
    plus, minus = pl.pallas_call(
        prepare_kernel,
        out_shape=(pair, pair),
        in_specs=[SMEM, ANY],
        out_specs=(ANY, ANY),
        scratch_shapes=[pltpu.SemaphoreType.DMA((4,))],
        compiler_params=pltpu.CompilerParams(vmem_limit_bytes=60 * 1024 * 1024),
        cost_estimate=cost(0, 1),
    )(place, blocks)
    from_left = shifted(plus, 1)
    from_right = shifted(minus, -1)
    old_pieces = root_prev.reshape(workers, size // workers, size)
    initial = lax.all_to_all(old_pieces, "mp", split_axis=0, concat_axis=0, tiled=True).reshape(size, size)

    def piece(slot):
        return pl.BlockSpec((None, half, size), lambda i, place: (slot, 0, 0))

    def own(step, row, rows):
        return pl.BlockSpec((1, rows, size), lambda i, place: ((place[0] + step) % ring, row, 0))

    whole = pl.BlockSpec((half, size), lambda i, place: (0, 0))
    upper, lower = pl.pallas_call(
        relay_kernel,
        out_shape=(part, part),
        grid_spec=pltpu.PrefetchScalarGridSpec(
            num_scalar_prefetch=1,
            grid=(1,),
            in_specs=[own(1, 0, half), own(3, 1, half), piece(0), piece(0)],
            out_specs=(whole, whole),
        ),
        compiler_params=PARAMS,
        cost_estimate=cost(0, 1),
    )(place, blocks, blocks, from_left, from_right)
    upper, lower = shifted(upper, 1), shifted(lower, -1)
    mine = pl.pallas_call(
        finish_kernel,
        out_shape=matrix,
        grid_spec=pltpu.PrefetchScalarGridSpec(
            num_scalar_prefetch=1,
            grid=(1,),
            in_specs=[own(0, 0, size), piece(1), piece(1), whole, whole],
            out_specs=pl.BlockSpec((size, size), lambda i, place: (0, 0)),
        ),
        compiler_params=PARAMS,
        cost_estimate=cost(0, 1),
    )(place, blocks, from_left, from_right, upper, lower)
    other = lax.ppermute(mine, "dp", [(i, i ^ 1) for i in range(replicas)])

    flops = 2 * size**3
    high, low = pl.pallas_call(
        fifth_kernel,
        out_shape=(matrix, matrix),
        in_specs=[VMEM],
        out_specs=(VMEM, VMEM),
        compiler_params=PARAMS,
        cost_estimate=cost(6 * flops, 6 * size**2),
    )(initial)
    fresh, refined = pl.pallas_call(
        refresh_kernel,
        out_shape=(jax.ShapeDtypeStruct((size, size), jnp.float32), matrix),
        in_specs=[SMEM] + [VMEM] * 6,
        out_specs=(VMEM, VMEM),
        compiler_params=PARAMS,
        cost_estimate=cost(4 * flops, 22 * size**2),
    )(side.reshape(1), mine, other, factors[0, 0], initial, high, low)

    pieces = lax.all_to_all(refined.reshape(old_pieces.shape), "mp", split_axis=0, concat_axis=0, tiled=True)
    refresh = plan[0] < workers
    new_roots = jnp.where(refresh[:, None, None], pieces, old_pieces).reshape(root_prev.shape)
    return fresh[None, None], new_roots


def solution(mesh):
    return jax.shard_map(
        local,
        mesh=mesh,
        in_specs=(
            P("dp", "mp", None, None, None),
            P("mp", "dp", None, None),
            P(None, "dp", "mp", None),
            P("dp", None),
        ),
        out_specs=(P("mp", "dp", None, None), P(None, "dp", "mp", None)),
        check_vma=False,
    )
```

```python
import jax
import jax.numpy as jnp
from jax import lax
from jax.experimental import pallas as pl
from jax.experimental.pallas import tpu as pltpu
from jax.sharding import PartitionSpec as P

keep_rate = 0.8
VMEM = pl.BlockSpec(memory_space=pltpu.VMEM)
ANY = pl.BlockSpec(memory_space=pl.ANY)
SMEM = pl.BlockSpec(memory_space=pltpu.SMEM)
PARAMS = pltpu.CompilerParams(vmem_limit_bytes=20 * 1024 * 1024)


def dot(a, b):
    return jnp.dot(a, b, preferred_element_type=jnp.float32)


def split(value):
    high = value.astype(jnp.bfloat16)
    return high, (value - high.astype(jnp.float32)).astype(jnp.bfloat16)


def fifth_kernel(root_ref, high_ref, low_ref):
    root = root_ref[...]
    high, low = split(dot(root, root))
    high, low = split(dot(high, high) + (dot(high, low) + dot(low, high)))
    high_ref[...], low_ref[...] = split(dot(root, high) + dot(root, low))


def prepare_kernel(x_ref, relay_up_ref, right_ref, relay_low_ref, left_ref, plus_ref, minus_ref):
    plus_ref[0], plus_ref[1] = relay_up_ref[0], right_ref[0]
    minus_ref[0], minus_ref[1] = relay_low_ref[0], left_ref[0]


def add(*values):
    return sum(value.astype(jnp.float32) for value in values).astype(jnp.bfloat16)


def relay_kernel(x_ref, right_ref, left_ref, from_left_ref, from_right_ref, upper_ref, lower_ref):
    upper_ref[...] = add(right_ref[0], from_left_ref[...])
    lower_ref[...] = add(left_ref[0], from_right_ref[...])


def finish_kernel(x_ref, own_ref, from_left_ref, from_right_ref, upper_ref, lower_ref, mine_ref):
    half = upper_ref.shape[0]
    mine_ref[:half] = add(own_ref[0, :half], from_right_ref[...], upper_ref[...])
    mine_ref[half:] = add(own_ref[0, half:], from_left_ref[...], lower_ref[...])


def refresh_kernel(side_ref, mine_ref, other_ref, factor_ref, root_ref, high_ref, low_ref, fresh_ref, refined_ref):
    summed = add(mine_ref[...], other_ref[...])

    def update(gram):
        fresh_ref[...] = keep_rate * factor_ref[...] + (1.0 - keep_rate) * gram

    @pl.when(side_ref[0] == 0)
    def _():
        update(lax.dot_general(summed, summed, (((1,), (1,)), ((), ())), preferred_element_type=jnp.float32))

    @pl.when(side_ref[0] != 0)
    def _():
        update(lax.dot_general(summed, summed, (((0,), (0,)), ((), ())), preferred_element_type=jnp.float32))

    high, low = split(fresh_ref[...])
    coupled = dot(high_ref[...], high) + (dot(high_ref[...], low) + dot(low_ref[...], high))
    refined_ref[...] = (1.25 * root_ref[...].astype(jnp.float32) - 0.25 * coupled).astype(jnp.bfloat16)


def cost(flops, moved):
    return pl.CostEstimate(flops=flops, bytes_accessed=moved, transcendentals=0)


def local(grad_parts, factors, root_prev, plan):
    workers = lax.axis_size("mp")
    replicas = lax.axis_size("dp")
    size = factors.shape[-1]
    half = size // 2
    blocks = grad_parts[0, 0]
    ring = blocks.shape[0]
    dp = lax.axis_index("dp")
    x, side = dp // 2, dp % 2

    def shifted(value, step):
        return lax.ppermute(value, "dp", [(i, (i // 2 + step) % ring * 2 + i % 2) for i in range(replicas)])

    pair = jax.ShapeDtypeStruct((2, half, size), jnp.bfloat16)
    part = jax.ShapeDtypeStruct((half, size), jnp.bfloat16)
    matrix = jax.ShapeDtypeStruct((size, size), jnp.bfloat16)
    place = x.reshape(1)

    def piece(slot):
        return pl.BlockSpec((None, half, size), lambda i, place: (slot, 0, 0))

    def own(step, row, rows):
        return pl.BlockSpec((1, rows, size), lambda i, place: ((place[0] + step) % ring, row, 0))

    both = pl.BlockSpec((2, half, size), lambda i, place: (0, 0, 0))
    plus, minus = pl.pallas_call(
        prepare_kernel,
        out_shape=(pair, pair),
        grid_spec=pltpu.PrefetchScalarGridSpec(
            num_scalar_prefetch=1,
            grid=(1,),
            in_specs=[own(2, 0, half), own(1, 1, half), own(2, 1, half), own(3, 0, half)],
            out_specs=(both, both),
        ),
        compiler_params=pltpu.CompilerParams(vmem_limit_bytes=60 * 1024 * 1024),
        cost_estimate=cost(0, 1),
    )(place, blocks, blocks, blocks, blocks)
    from_left = shifted(plus, 1)
    from_right = shifted(minus, -1)
    old_pieces = root_prev.reshape(workers, size // workers, size)
    initial = lax.all_to_all(old_pieces, "mp", split_axis=0, concat_axis=0, tiled=True).reshape(size, size)

    whole = pl.BlockSpec((half, size), lambda i, place: (0, 0))
    upper, lower = pl.pallas_call(
        relay_kernel,
        out_shape=(part, part),
        grid_spec=pltpu.PrefetchScalarGridSpec(
            num_scalar_prefetch=1,
            grid=(1,),
            in_specs=[own(1, 0, half), own(3, 1, half), piece(0), piece(0)],
            out_specs=(whole, whole),
        ),
        compiler_params=PARAMS,
        cost_estimate=cost(0, 1),
    )(place, blocks, blocks, from_left, from_right)
    upper, lower = shifted(upper, 1), shifted(lower, -1)
    mine = pl.pallas_call(
        finish_kernel,
        out_shape=matrix,
        grid_spec=pltpu.PrefetchScalarGridSpec(
            num_scalar_prefetch=1,
            grid=(1,),
            in_specs=[own(0, 0, size), piece(1), piece(1), whole, whole],
            out_specs=pl.BlockSpec((size, size), lambda i, place: (0, 0)),
        ),
        compiler_params=PARAMS,
        cost_estimate=cost(0, 1),
    )(place, blocks, from_left, from_right, upper, lower)
    other = lax.ppermute(mine, "dp", [(i, i ^ 1) for i in range(replicas)])

    flops = 2 * size**3
    high, low = pl.pallas_call(
        fifth_kernel,
        out_shape=(matrix, matrix),
        in_specs=[VMEM],
        out_specs=(VMEM, VMEM),
        compiler_params=PARAMS,
        cost_estimate=cost(6 * flops, 6 * size**2),
    )(initial)
    fresh, refined = pl.pallas_call(
        refresh_kernel,
        out_shape=(jax.ShapeDtypeStruct((size, size), jnp.float32), matrix),
        in_specs=[SMEM] + [VMEM] * 6,
        out_specs=(VMEM, VMEM),
        compiler_params=PARAMS,
        cost_estimate=cost(4 * flops, 22 * size**2),
    )(side.reshape(1), mine, other, factors[0, 0], initial, high, low)

    pieces = lax.all_to_all(refined.reshape(old_pieces.shape), "mp", split_axis=0, concat_axis=0, tiled=True)
    refresh = plan[0] < workers
    new_roots = jnp.where(refresh[:, None, None], pieces, old_pieces).reshape(root_prev.shape)
    return fresh[None, None], new_roots


def solution(mesh):
    return jax.shard_map(
        local,
        mesh=mesh,
        in_specs=(
            P("dp", "mp", None, None, None),
            P("mp", "dp", None, None),
            P(None, "dp", "mp", None),
            P("dp", None),
        ),
        out_specs=(P("mp", "dp", None, None), P(None, "dp", "mp", None)),
        check_vma=False,
    )
```

```python
import jax
import jax.numpy as jnp
from jax import lax
from jax.experimental import pallas as pl
from jax.experimental.pallas import tpu as pltpu
from jax.sharding import PartitionSpec as P

keep_rate = 0.8
VMEM = pl.BlockSpec(memory_space=pltpu.VMEM)
ANY = pl.BlockSpec(memory_space=pl.ANY)
SMEM = pl.BlockSpec(memory_space=pltpu.SMEM)
PARAMS = pltpu.CompilerParams(vmem_limit_bytes=20 * 1024 * 1024)


def dot(a, b):
    return jnp.dot(a, b, preferred_element_type=jnp.float32)


def split(value):
    high = value.astype(jnp.bfloat16)
    return high, (value - high.astype(jnp.float32)).astype(jnp.bfloat16)


def fifth_kernel(root_ref, high_ref, low_ref):
    root = root_ref[...]
    high, low = split(dot(root, root))
    high, low = split(dot(high, high) + (dot(high, low) + dot(low, high)))
    high_ref[...], low_ref[...] = split(dot(root, high) + dot(root, low))


def add(*values):
    return sum(value.astype(jnp.float32) for value in values).astype(jnp.bfloat16)


def chip_kernel(place_ref, *refs):
    ring = len(refs) // 3
    for k in range(ring):
        refs[2 * ring + k][...] = add(refs[k][0], refs[ring + k][0])


def finish_kernel(*refs):
    refs[-1][...] = add(*[ref[...] for ref in refs[:-1]])


def refresh_kernel(side_ref, mine_ref, other_ref, factor_ref, root_ref, high_ref, low_ref, fresh_ref, refined_ref):
    summed = jnp.concatenate([mine_ref[...], other_ref[...]], axis=0)

    def update(gram):
        fresh_ref[...] = keep_rate * factor_ref[...] + (1.0 - keep_rate) * gram

    @pl.when(side_ref[0] == 0)
    def _():
        update(lax.dot_general(summed, summed, (((1,), (1,)), ((), ())), preferred_element_type=jnp.float32))

    @pl.when(side_ref[0] != 0)
    def _():
        update(lax.dot_general(summed, summed, (((0,), (0,)), ((), ())), preferred_element_type=jnp.float32))

    high, low = split(fresh_ref[...])
    coupled = dot(high_ref[...], high) + (dot(high_ref[...], low) + dot(low_ref[...], high))
    refined_ref[...] = (1.25 * root_ref[...].astype(jnp.float32) - 0.25 * coupled).astype(jnp.bfloat16)


def cost(flops, moved):
    return pl.CostEstimate(flops=flops, bytes_accessed=moved, transcendentals=0)


def local(grad_parts, factors, root_prev, plan):
    workers = lax.axis_size("mp")
    replicas = lax.axis_size("dp")
    size = factors.shape[-1]
    half = size // 2
    blocks = grad_parts[0, 0]
    ring = blocks.shape[0]
    dp = lax.axis_index("dp")
    x, side = dp // 2, dp % 2

    def swapped(value):
        return lax.ppermute(value, "dp", [(i, i ^ 1) for i in range(replicas)])

    def around(value, step):
        pairs = [(i, (i // 2 + (1 - 2 * (i % 2)) * step) % ring * 2 + i % 2) for i in range(replicas)]
        return lax.ppermute(value, "dp", pairs)

    theirs = swapped(blocks)
    old_pieces = root_prev.reshape(workers, size // workers, size)
    initial = lax.all_to_all(old_pieces, "mp", split_axis=0, concat_axis=0, tiled=True).reshape(size, size)

    matrix = jax.ShapeDtypeStruct((size, size), jnp.bfloat16)
    part = jax.ShapeDtypeStruct((half, size), jnp.bfloat16)

    def my_half(step):
        def index(i, place):
            return (place[0] + (1 - 2 * place[1]) * step + ring) % ring, place[1], 0

        return pl.BlockSpec((1, half, size), index)

    specs = [my_half(step) for step in range(ring)]
    sums = pl.pallas_call(
        chip_kernel,
        out_shape=(part,) * ring,
        grid_spec=pltpu.PrefetchScalarGridSpec(
            num_scalar_prefetch=1,
            grid=(1,),
            in_specs=specs * 2,
            out_specs=(pl.BlockSpec((half, size), lambda i, place: (0, 0)),) * ring,
        ),
        compiler_params=PARAMS,
        cost_estimate=cost(0, 1),
    )(jnp.stack([x, side]), *[blocks] * ring, *[theirs] * ring)
    received = [around(sums[step], step) for step in range(1, ring)]
    mine = pl.pallas_call(
        finish_kernel,
        out_shape=part,
        in_specs=[VMEM] * ring,
        out_specs=VMEM,
        compiler_params=PARAMS,
        cost_estimate=cost(0, 1),
    )(sums[0], *received)
    other = swapped(mine)

    flops = 2 * size**3
    high, low = pl.pallas_call(
        fifth_kernel,
        out_shape=(matrix, matrix),
        in_specs=[VMEM],
        out_specs=(VMEM, VMEM),
        compiler_params=PARAMS,
        cost_estimate=cost(6 * flops, 6 * size**2),
    )(initial)
    fresh, refined = pl.pallas_call(
        refresh_kernel,
        out_shape=(jax.ShapeDtypeStruct((size, size), jnp.float32), matrix),
        in_specs=[SMEM] + [VMEM] * 6,
        out_specs=(VMEM, VMEM),
        compiler_params=PARAMS,
        cost_estimate=cost(4 * flops, 22 * size**2),
    )(side.reshape(1), mine, other, factors[0, 0], initial, high, low)

    fresh_roots = lax.all_to_all(refined.reshape(old_pieces.shape), "mp", split_axis=0, concat_axis=0, tiled=True)
    refresh = plan[0] < workers
    new_roots = jnp.where(refresh[:, None, None], fresh_roots, old_pieces).reshape(root_prev.shape)
    return fresh[None, None], new_roots


def solution(mesh):
    return jax.shard_map(
        local,
        mesh=mesh,
        in_specs=(
            P("dp", "mp", None, None, None),
            P("mp", "dp", None, None),
            P(None, "dp", "mp", None),
            P("dp", None),
        ),
        out_specs=(P("mp", "dp", None, None), P(None, "dp", "mp", None)),
        check_vma=False,
    )
```

```python
import jax
import jax.numpy as jnp
from jax import lax
from jax.experimental import pallas as pl
from jax.experimental.pallas import tpu as pltpu
from jax.sharding import PartitionSpec as P

keep_rate = 0.8
VMEM = pl.BlockSpec(memory_space=pltpu.VMEM)
ANY = pl.BlockSpec(memory_space=pl.ANY)
SMEM = pl.BlockSpec(memory_space=pltpu.SMEM)
PARAMS = pltpu.CompilerParams(vmem_limit_bytes=20 * 1024 * 1024)


def dot(a, b):
    return jnp.dot(a, b, preferred_element_type=jnp.float32)


def split(value):
    high = value.astype(jnp.bfloat16)
    return high, (value - high.astype(jnp.float32)).astype(jnp.bfloat16)


def fifth_kernel(root_ref, high_ref, low_ref):
    root = root_ref[...]
    high, low = split(dot(root, root))
    high, low = split(dot(high, high) + (dot(high, low) + dot(low, high)))
    high_ref[...], low_ref[...] = split(dot(root, high) + dot(root, low))


def add(*values):
    return sum(value.astype(jnp.float32) for value in values).astype(jnp.bfloat16)


def refresh_kernel(side_ref, mine_ref, other_ref, factor_ref, root_ref, high_ref, low_ref, fresh_ref, refined_ref):
    summed = add(mine_ref[...], other_ref[...])

    def update(gram):
        fresh_ref[...] = keep_rate * factor_ref[...] + (1.0 - keep_rate) * gram

    @pl.when(side_ref[0] == 0)
    def _():
        update(lax.dot_general(summed, summed, (((1,), (1,)), ((), ())), preferred_element_type=jnp.float32))

    @pl.when(side_ref[0] != 0)
    def _():
        update(lax.dot_general(summed, summed, (((0,), (0,)), ((), ())), preferred_element_type=jnp.float32))

    high, low = split(fresh_ref[...])
    coupled = dot(high_ref[...], high) + (dot(high_ref[...], low) + dot(low_ref[...], high))
    refined_ref[...] = (1.25 * root_ref[...].astype(jnp.float32) - 0.25 * coupled).astype(jnp.bfloat16)


def cost(flops, moved):
    return pl.CostEstimate(flops=flops, bytes_accessed=moved, transcendentals=0)


def local(grad_parts, factors, root_prev, plan):
    workers = lax.axis_size("mp")
    replicas = lax.axis_size("dp")
    size = factors.shape[-1]
    blocks = grad_parts[0, 0]
    ring = blocks.shape[0]
    dp = lax.axis_index("dp")
    x, side = dp // 2, dp % 2

    def swapped(value):
        return lax.ppermute(value, "dp", [(i, i ^ 1) for i in range(replicas)])

    def block(values, step):
        return lax.dynamic_index_in_dim(values, (x + step + ring) % ring, 0, keepdims=False)

    theirs = swapped(blocks)
    opposite = [(i, (i // 2 + 2) % ring * 2 + i % 2) for i in range(replicas)]
    from_opposite = lax.ppermute(block(blocks, 2), "dp", opposite)
    old_pieces = root_prev.reshape(workers, size // workers, size)
    initial = lax.all_to_all(old_pieces, "mp", split_axis=0, concat_axis=0, tiled=True).reshape(size, size)

    theirs, from_opposite = lax.optimization_barrier((theirs, from_opposite))
    ahead = 1 - 2 * side
    for_next = add(block(blocks, ahead), block(theirs, ahead))
    onward = [(i, (i // 2 + 1 - 2 * (i % 2)) % ring * 2 + i % 2) for i in range(replicas)]
    cut = size * 3 // 4
    from_last = jnp.concatenate([lax.ppermute(rows, "dp", onward) for rows in (for_next[:cut], for_next[cut:])])
    mine = add(block(blocks, 0), from_opposite, from_last)
    other = swapped(mine)

    matrix = jax.ShapeDtypeStruct((size, size), jnp.bfloat16)
    flops = 2 * size**3
    high, low = pl.pallas_call(
        fifth_kernel,
        out_shape=(matrix, matrix),
        in_specs=[VMEM],
        out_specs=(VMEM, VMEM),
        compiler_params=PARAMS,
        cost_estimate=cost(6 * flops, 6 * size**2),
    )(initial)
    fresh, refined = pl.pallas_call(
        refresh_kernel,
        out_shape=(jax.ShapeDtypeStruct((size, size), jnp.float32), matrix),
        in_specs=[SMEM] + [VMEM] * 6,
        out_specs=(VMEM, VMEM),
        compiler_params=PARAMS,
        cost_estimate=cost(4 * flops, 22 * size**2),
    )(side.reshape(1), mine, other, factors[0, 0], initial, high, low)

    fresh_roots = lax.all_to_all(refined.reshape(old_pieces.shape), "mp", split_axis=0, concat_axis=0, tiled=True)
    refresh = plan[0] < workers
    new_roots = jnp.where(refresh[:, None, None], fresh_roots, old_pieces).reshape(root_prev.shape)
    return fresh[None, None], new_roots


def solution(mesh):
    return jax.shard_map(
        local,
        mesh=mesh,
        in_specs=(
            P("dp", "mp", None, None, None),
            P("mp", "dp", None, None),
            P(None, "dp", "mp", None),
            P("dp", None),
        ),
        out_specs=(P("mp", "dp", None, None), P(None, "dp", "mp", None)),
        check_vma=False,
    )
```

```python
import jax
import jax.numpy as jnp
from jax import lax
from jax.experimental import pallas as pl
from jax.experimental.pallas import tpu as pltpu
from jax.sharding import PartitionSpec as P

keep_rate = 0.8
VMEM = pl.BlockSpec(memory_space=pltpu.VMEM)
HBM = pl.BlockSpec(memory_space=pltpu.HBM)
SMEM = pl.BlockSpec(memory_space=pltpu.SMEM)
PARAMS = pltpu.CompilerParams(vmem_limit_bytes=20 * 1024 * 1024)


def dot(a, b):
    return jnp.dot(a, b, preferred_element_type=jnp.float32)


def split(value):
    high = value.astype(jnp.bfloat16)
    return high, (value - high.astype(jnp.float32)).astype(jnp.bfloat16)


def base_kernel(root_ref, factor_ref, fifth_ref, base_ref, old, sem):
    load = pltpu.make_async_copy(factor_ref, old, sem)
    load.start()
    root = root_ref[...]
    high, low = split(dot(root, root))
    high, low = split(dot(high, high) + (dot(high, low) + dot(low, high)))
    high, low = split(dot(root, high) + dot(root, low))
    fifth_ref[...] = high
    load.wait()
    factor, rest = split(old[...])
    coupled = dot(high, factor) + (dot(high, rest) + dot(low, factor))
    base_ref[...] = 1.25 * root.astype(jnp.float32) - 0.25 * keep_rate * coupled


def add(*values):
    return sum(value.astype(jnp.float32) for value in values).astype(jnp.bfloat16)


def chip_kernel(place_ref, *refs):
    ring = len(refs) // 3
    for k in range(ring):
        refs[2 * ring + k][...] = add(refs[k][0], refs[ring + k][0])


def finish_kernel(*refs):
    refs[-1][...] = add(*[ref[...] for ref in refs[:-1]])


def refresh_kernel(dp_ref, mine_ref, other_ref, factor_ref, fifth_ref, base_ref, fresh_ref, refined_ref, old, held, sems):
    load = pltpu.make_async_copy(factor_ref, old, sems.at[0])
    store = pltpu.make_async_copy(held, fresh_ref, sems.at[1])
    load.start()
    summed = jnp.concatenate([mine_ref[...], other_ref[...]], axis=0)

    def update(contract):
        gram = lax.dot_general(summed, summed, (((contract,), (contract,)), ((), ())), preferred_element_type=jnp.float32)
        load.wait()
        held[...] = keep_rate * old[...] + (1.0 - keep_rate) * gram
        store.start()
        coupled = dot(fifth_ref[...], gram.astype(jnp.bfloat16))
        refined_ref[...] = (base_ref[...] - 0.25 * (1.0 - keep_rate) * coupled).astype(jnp.bfloat16)

    @pl.when(lax.rem(dp_ref[0], 2) == 0)
    def _():
        update(1)

    @pl.when(lax.rem(dp_ref[0], 2) != 0)
    def _():
        update(0)

    store.wait()


def cost(flops, moved):
    return pl.CostEstimate(flops=flops, bytes_accessed=moved, transcendentals=0)


def local(grad_parts, factors, root_prev, plan):
    workers = lax.axis_size("mp")
    replicas = lax.axis_size("dp")
    size = factors.shape[-1]
    half = size // 2
    blocks = grad_parts[0, 0]
    ring = blocks.shape[0]
    dp = lax.axis_index("dp")

    def swapped(value):
        return lax.ppermute(value, "dp", [(i, i ^ 1) for i in range(replicas)])

    def around(value, step):
        pairs = [(i, (i // 2 + (1 - 2 * (i % 2)) * step) % ring * 2 + i % 2) for i in range(replicas)]
        return lax.ppermute(value, "dp", pairs)

    theirs = swapped(blocks)
    old_pieces = root_prev.reshape(workers, size // workers, size)
    initial = lax.all_to_all(old_pieces, "mp", split_axis=0, concat_axis=0, tiled=True).reshape(size, size)

    matrix = jax.ShapeDtypeStruct((size, size), jnp.bfloat16)
    part = jax.ShapeDtypeStruct((half, size), jnp.bfloat16)

    def my_half(step):
        def index(i, place):
            core = lax.rem(place[0], 2)
            return lax.rem(lax.div(place[0], 2) + (1 - 2 * core) * step + ring, ring), core, 0

        return pl.BlockSpec((1, half, size), index)

    held = pltpu.with_memory_space_constraint(blocks, pltpu.HBM)
    specs = [my_half(step) for step in range(ring)]
    sums = pl.pallas_call(
        chip_kernel,
        out_shape=(part,) * ring,
        grid_spec=pltpu.PrefetchScalarGridSpec(
            num_scalar_prefetch=1,
            grid=(1,),
            in_specs=specs * 2,
            out_specs=(pl.BlockSpec((half, size), lambda i, place: (0, 0)),) * ring,
        ),
        compiler_params=PARAMS,
        cost_estimate=cost(0, 1),
    )(dp.reshape(1), *[held] * ring, *[theirs] * ring)
    received = [around(sums[step], step) for step in (2, 1, 3)]
    mine = pl.pallas_call(
        finish_kernel,
        out_shape=part,
        in_specs=[VMEM] * ring,
        out_specs=VMEM,
        compiler_params=PARAMS,
        cost_estimate=cost(0, 1),
    )(sums[0], *received)
    other = swapped(mine)

    flops = 2 * size**3
    old_factor = pltpu.with_memory_space_constraint(factors[0, 0], pltpu.HBM)
    whole = jax.ShapeDtypeStruct((size, size), jnp.float32)
    fifth, base = pl.pallas_call(
        base_kernel,
        out_shape=(matrix, whole),
        in_specs=[VMEM, HBM],
        out_specs=(VMEM, VMEM),
        scratch_shapes=[pltpu.VMEM((size, size), jnp.float32), pltpu.SemaphoreType.DMA],
        compiler_params=PARAMS,
        cost_estimate=cost(9 * flops, 12 * size**2),
    )(initial, old_factor)
    fresh, refined = pl.pallas_call(
        refresh_kernel,
        out_shape=(whole, matrix),
        in_specs=[SMEM, VMEM, VMEM, HBM, VMEM, VMEM],
        out_specs=(HBM, VMEM),
        scratch_shapes=[pltpu.VMEM((size, size), jnp.float32)] * 2 + [pltpu.SemaphoreType.DMA((2,))],
        compiler_params=PARAMS,
        cost_estimate=cost(2 * flops, 16 * size**2),
    )(dp.reshape(1), mine, other, old_factor, fifth, base)

    fresh_roots = lax.all_to_all(refined.reshape(old_pieces.shape), "mp", split_axis=0, concat_axis=0, tiled=True)
    refresh = plan[0] < workers
    new_roots = jnp.where(refresh[:, None, None], fresh_roots, old_pieces).reshape(root_prev.shape)
    return fresh[None, None], new_roots


def solution(mesh):
    return jax.shard_map(
        local,
        mesh=mesh,
        in_specs=(
            P("dp", "mp", None, None, None),
            P("mp", "dp", None, None),
            P(None, "dp", "mp", None),
            P("dp", None),
        ),
        out_specs=(P("mp", "dp", None, None), P(None, "dp", "mp", None)),
        check_vma=False,
    )
```

```python
import jax
import jax.numpy as jnp
from jax import lax
from jax.experimental import pallas as pl
from jax.experimental.pallas import tpu as pltpu
from jax.sharding import PartitionSpec as P

keep_rate = 0.8
VMEM = pl.BlockSpec(memory_space=pltpu.VMEM)
HBM = pl.BlockSpec(memory_space=pltpu.HBM)
SMEM = pl.BlockSpec(memory_space=pltpu.SMEM)
PARAMS = pltpu.CompilerParams(vmem_limit_bytes=20 * 1024 * 1024)


def dot(a, b):
    return jnp.dot(a, b, preferred_element_type=jnp.float32)


def split(value):
    high = value.astype(jnp.bfloat16)
    return high, (value - high.astype(jnp.float32)).astype(jnp.bfloat16)


def base_kernel(root_ref, factor_ref, fifth_ref, base_ref, old, sem):
    load = pltpu.make_async_copy(factor_ref, old, sem)
    load.start()
    root = root_ref[...]
    high, low = split(dot(root, root))
    high, low = split(dot(high, high) + (dot(high, low) + dot(low, high)))
    high, low = split(dot(root, high) + dot(root, low))
    fifth_ref[...] = high
    load.wait()
    factor, rest = split(old[...])
    coupled = dot(high, factor) + (dot(high, rest) + dot(low, factor))
    base_ref[...] = 1.25 * root.astype(jnp.float32) - 0.25 * keep_rate * coupled


def add(*values):
    return sum(value.astype(jnp.float32) for value in values).astype(jnp.bfloat16)


def chip_kernel(place_ref, *refs):
    ring = len(refs) // 3
    for k in range(ring):
        refs[2 * ring + k][...] = add(refs[k][0], refs[ring + k][0])


def finish_kernel(*refs):
    refs[-1][...] = add(*[ref[...] for ref in refs[:-1]])


def refresh_kernel(dp_ref, mine_ref, other_ref, factor_ref, fifth_ref, base_ref, fresh_ref, refined_ref):
    summed = jnp.concatenate([mine_ref[...], other_ref[...]], axis=0)

    def update(contract):
        gram = lax.dot_general(summed, summed, (((contract,), (contract,)), ((), ())), preferred_element_type=jnp.float32)
        fresh_ref[...] = keep_rate * factor_ref[...] + (1.0 - keep_rate) * gram
        coupled = dot(fifth_ref[...], gram.astype(jnp.bfloat16))
        refined_ref[...] = (base_ref[...] - 0.25 * (1.0 - keep_rate) * coupled).astype(jnp.bfloat16)

    @pl.when(lax.rem(dp_ref[0], 2) == 0)
    def _():
        update(1)

    @pl.when(lax.rem(dp_ref[0], 2) != 0)
    def _():
        update(0)


def cost(flops, moved):
    return pl.CostEstimate(flops=flops, bytes_accessed=moved, transcendentals=0)


def local(grad_parts, factors, root_prev, plan):
    workers = lax.axis_size("mp")
    replicas = lax.axis_size("dp")
    size = factors.shape[-1]
    half = size // 2
    blocks = grad_parts[0, 0]
    ring = blocks.shape[0]
    dp = lax.axis_index("dp")

    def swapped(value):
        return lax.ppermute(value, "dp", [(i, i ^ 1) for i in range(replicas)])

    def around(value, step):
        pairs = [(i, (i // 2 + (1 - 2 * (i % 2)) * step) % ring * 2 + i % 2) for i in range(replicas)]
        return lax.ppermute(value, "dp", pairs)

    theirs = swapped(blocks)
    old_pieces = root_prev.reshape(workers, size // workers, size)
    initial = lax.all_to_all(old_pieces, "mp", split_axis=0, concat_axis=0, tiled=True).reshape(size, size)

    matrix = jax.ShapeDtypeStruct((size, size), jnp.bfloat16)
    part = jax.ShapeDtypeStruct((half, size), jnp.bfloat16)

    def my_half(step):
        def index(i, place):
            core = lax.rem(place[0], 2)
            return lax.rem(lax.div(place[0], 2) + (1 - 2 * core) * step + ring, ring), core, 0

        return pl.BlockSpec((1, half, size), index)

    held = pltpu.with_memory_space_constraint(blocks, pltpu.HBM)
    specs = [my_half(step) for step in range(ring)]
    sums = pl.pallas_call(
        chip_kernel,
        out_shape=(part,) * ring,
        grid_spec=pltpu.PrefetchScalarGridSpec(
            num_scalar_prefetch=1,
            grid=(1,),
            in_specs=specs * 2,
            out_specs=(pl.BlockSpec((half, size), lambda i, place: (0, 0)),) * ring,
        ),
        compiler_params=PARAMS,
        cost_estimate=cost(0, 1),
    )(dp.reshape(1), *[held] * ring, *[theirs] * ring)
    received = [around(sums[step], step) for step in range(1, ring)]
    flops = 2 * size**3
    old_factor = pltpu.with_memory_space_constraint(factors[0, 0], pltpu.HBM)
    whole = jax.ShapeDtypeStruct((size, size), jnp.float32)
    fifth, base = pl.pallas_call(
        base_kernel,
        out_shape=(matrix, whole),
        in_specs=[VMEM, HBM],
        out_specs=(VMEM, VMEM),
        scratch_shapes=[pltpu.VMEM((size, size), jnp.float32), pltpu.SemaphoreType.DMA],
        compiler_params=PARAMS,
        cost_estimate=cost(9 * flops, 12 * size**2),
    )(initial, old_factor)
    fifth, base, *received = lax.optimization_barrier((fifth, base, *received))
    mine = pl.pallas_call(
        finish_kernel,
        out_shape=part,
        in_specs=[VMEM] * ring,
        out_specs=VMEM,
        compiler_params=PARAMS,
        cost_estimate=cost(0, 1),
    )(sums[0], *received)
    other = swapped(mine)

    fresh, refined = pl.pallas_call(
        refresh_kernel,
        out_shape=(whole, matrix),
        in_specs=[SMEM] + [VMEM] * 5,
        out_specs=(VMEM, VMEM),
        compiler_params=PARAMS,
        cost_estimate=cost(2 * flops, 16 * size**2),
    )(dp.reshape(1), mine, other, factors[0, 0], fifth, base)

    fresh_roots = lax.all_to_all(refined.reshape(old_pieces.shape), "mp", split_axis=0, concat_axis=0, tiled=True)
    refresh = plan[0] < workers
    new_roots = jnp.where(refresh[:, None, None], fresh_roots, old_pieces).reshape(root_prev.shape)
    return fresh[None, None], new_roots


def solution(mesh):
    return jax.shard_map(
        local,
        mesh=mesh,
        in_specs=(
            P("dp", "mp", None, None, None),
            P("mp", "dp", None, None),
            P(None, "dp", "mp", None),
            P("dp", None),
        ),
        out_specs=(P("mp", "dp", None, None), P(None, "dp", "mp", None)),
        check_vma=False,
    )
```

```python
import jax
import jax.numpy as jnp
from jax import lax
from jax.experimental import pallas as pl
from jax.experimental.pallas import tpu as pltpu
from jax.sharding import PartitionSpec as P

keep_rate = 0.8
VMEM = pl.BlockSpec(memory_space=pltpu.VMEM)
HBM = pl.BlockSpec(memory_space=pltpu.HBM)
SMEM = pl.BlockSpec(memory_space=pltpu.SMEM)
PARAMS = pltpu.CompilerParams(vmem_limit_bytes=20 * 1024 * 1024)


def dot(a, b):
    return jnp.dot(a, b, preferred_element_type=jnp.float32)


def split(value):
    high = value.astype(jnp.bfloat16)
    return high, (value - high.astype(jnp.float32)).astype(jnp.bfloat16)


def base_kernel(root_ref, factor_ref, fifth_ref, base_ref, old, sem):
    load = pltpu.make_async_copy(factor_ref, old, sem)
    load.start()
    root = root_ref[...]
    high, low = split(dot(root, root))
    high, low = split(dot(high, high) + (dot(high, low) + dot(low, high)))
    high, low = split(dot(root, high) + dot(root, low))
    fifth_ref[...] = high
    load.wait()
    factor, rest = split(old[...])
    coupled = dot(high, factor) + (dot(high, rest) + dot(low, factor))
    base_ref[...] = 1.25 * root.astype(jnp.float32) - 0.25 * keep_rate * coupled


def add(*values):
    return sum(value.astype(jnp.float32) for value in values).astype(jnp.bfloat16)


def chip_kernel(place_ref, *refs):
    ring = len(refs) // 3
    for k in range(ring):
        refs[2 * ring + k][...] = add(refs[k][0], refs[ring + k][0])


def finish_kernel(*refs):
    refs[-1][...] = add(*[ref[...] for ref in refs[:-1]])


def refine_kernel(dp_ref, mine_ref, other_ref, fifth_ref, base_ref, gram_ref, refined_ref):
    summed = jnp.concatenate([mine_ref[...], other_ref[...]], axis=0)

    def update(contract):
        gram = lax.dot_general(summed, summed, (((contract,), (contract,)), ((), ())), preferred_element_type=jnp.float32)
        gram_ref[...] = gram
        coupled = dot(fifth_ref[...], gram.astype(jnp.bfloat16))
        refined_ref[...] = (base_ref[...] - 0.25 * (1.0 - keep_rate) * coupled).astype(jnp.bfloat16)

    @pl.when(lax.rem(dp_ref[0], 2) == 0)
    def _():
        update(1)

    @pl.when(lax.rem(dp_ref[0], 2) != 0)
    def _():
        update(0)


def factor_kernel(factor_ref, gram_ref, fresh_ref):
    fresh_ref[...] = keep_rate * factor_ref[...] + (1.0 - keep_rate) * gram_ref[...]


def cost(flops, moved):
    return pl.CostEstimate(flops=flops, bytes_accessed=moved, transcendentals=0)


def local(grad_parts, factors, root_prev, plan):
    workers = lax.axis_size("mp")
    replicas = lax.axis_size("dp")
    size = factors.shape[-1]
    half = size // 2
    blocks = grad_parts[0, 0]
    ring = blocks.shape[0]
    dp = lax.axis_index("dp")

    def swapped(value):
        return lax.ppermute(value, "dp", [(i, i ^ 1) for i in range(replicas)])

    def around(value, step):
        pairs = [(i, (i // 2 + (1 - 2 * (i % 2)) * step) % ring * 2 + i % 2) for i in range(replicas)]
        return lax.ppermute(value, "dp", pairs)

    theirs = swapped(blocks)
    old_pieces = root_prev.reshape(workers, size // workers, size)
    initial = lax.all_to_all(old_pieces, "mp", split_axis=0, concat_axis=0, tiled=True).reshape(size, size)

    matrix = jax.ShapeDtypeStruct((size, size), jnp.bfloat16)
    part = jax.ShapeDtypeStruct((half, size), jnp.bfloat16)

    def my_half(step):
        def index(i, place):
            core = lax.rem(place[0], 2)
            return lax.rem(lax.div(place[0], 2) + (1 - 2 * core) * step + ring, ring), core, 0

        return pl.BlockSpec((1, half, size), index)

    held = pltpu.with_memory_space_constraint(blocks, pltpu.HBM)
    specs = [my_half(step) for step in range(ring)]
    sums = pl.pallas_call(
        chip_kernel,
        out_shape=(part,) * ring,
        grid_spec=pltpu.PrefetchScalarGridSpec(
            num_scalar_prefetch=1,
            grid=(1,),
            in_specs=specs * 2,
            out_specs=(pl.BlockSpec((half, size), lambda i, place: (0, 0)),) * ring,
        ),
        compiler_params=PARAMS,
        cost_estimate=cost(0, 1),
    )(dp.reshape(1), *[held] * ring, *[theirs] * ring)
    received = [around(sums[step], step) for step in range(1, ring)]
    flops = 2 * size**3
    old_factor = pltpu.with_memory_space_constraint(factors[0, 0], pltpu.HBM)
    whole = jax.ShapeDtypeStruct((size, size), jnp.float32)
    fifth, base = pl.pallas_call(
        base_kernel,
        out_shape=(matrix, whole),
        in_specs=[VMEM, HBM],
        out_specs=(VMEM, VMEM),
        scratch_shapes=[pltpu.VMEM((size, size), jnp.float32), pltpu.SemaphoreType.DMA],
        compiler_params=PARAMS,
        cost_estimate=cost(9 * flops, 12 * size**2),
    )(initial, old_factor)
    fifth, base, *received = lax.optimization_barrier((fifth, base, *received))
    mine = pl.pallas_call(
        finish_kernel,
        out_shape=part,
        in_specs=[VMEM] * ring,
        out_specs=VMEM,
        compiler_params=PARAMS,
        cost_estimate=cost(0, 1),
    )(sums[0], *received)
    other = swapped(mine)

    gram, refined = pl.pallas_call(
        refine_kernel,
        out_shape=(whole, matrix),
        in_specs=[SMEM] + [VMEM] * 4,
        out_specs=(VMEM, VMEM),
        compiler_params=PARAMS,
        cost_estimate=cost(2 * flops, 16 * size**2),
    )(dp.reshape(1), mine, other, fifth, base)
    fresh_roots = lax.all_to_all(refined.reshape(old_pieces.shape), "mp", split_axis=0, concat_axis=0, tiled=True)
    fresh = pl.pallas_call(
        factor_kernel,
        out_shape=whole,
        in_specs=[VMEM, VMEM],
        out_specs=VMEM,
        compiler_params=PARAMS,
        cost_estimate=cost(0, 12 * size**2),
    )(factors[0, 0], gram)
    refresh = plan[0] < workers
    new_roots = jnp.where(refresh[:, None, None], fresh_roots, old_pieces).reshape(root_prev.shape)
    return fresh[None, None], new_roots


def solution(mesh):
    return jax.shard_map(
        local,
        mesh=mesh,
        in_specs=(
            P("dp", "mp", None, None, None),
            P("mp", "dp", None, None),
            P(None, "dp", "mp", None),
            P("dp", None),
        ),
        out_specs=(P("mp", "dp", None, None), P(None, "dp", "mp", None)),
        check_vma=False,
    )
```

```python
import jax
import jax.numpy as jnp
from jax import lax
from jax.experimental import pallas as pl
from jax.experimental.pallas import tpu as pltpu
from jax.sharding import PartitionSpec as P

keep_rate = 0.8
VMEM = pl.BlockSpec(memory_space=pltpu.VMEM)
HBM = pl.BlockSpec(memory_space=pltpu.HBM)
SMEM = pl.BlockSpec(memory_space=pltpu.SMEM)
PARAMS = pltpu.CompilerParams(vmem_limit_bytes=20 * 1024 * 1024)


def dot(a, b):
    return jnp.dot(a, b, preferred_element_type=jnp.float32)


def split(value):
    high = value.astype(jnp.bfloat16)
    return high, (value - high.astype(jnp.float32)).astype(jnp.bfloat16)


def base_kernel(dp_ref, root_ref, factor_ref, blocks_ref, fifth_ref, base_ref, own_ref, old, sems):
    load = pltpu.make_async_copy(factor_ref, old, sems.at[0])
    load_own = pltpu.make_async_copy(blocks_ref.at[lax.div(dp_ref[0], 2)], own_ref, sems.at[1])
    load.start()
    load_own.start()
    root = root_ref[...]
    high, low = split(dot(root, root))
    high, low = split(dot(high, high) + (dot(high, low) + dot(low, high)))
    high, low = split(dot(root, high) + dot(root, low))
    fifth_ref[...] = high
    load.wait()
    factor, rest = split(old[...])
    coupled = dot(high, factor) + (dot(high, rest) + dot(low, factor))
    base_ref[...] = 1.25 * root.astype(jnp.float32) - 0.25 * keep_rate * coupled
    load_own.wait()


def add(*values):
    return sum(value.astype(jnp.float32) for value in values).astype(jnp.bfloat16)


def chip_kernel(dp_ref, next_ref, next_other_ref, far_ref, far_other_ref, next_out_ref, far_out_ref):
    far_out_ref[...] = add(far_ref[0], far_other_ref[0])
    next_out_ref[...] = add(next_ref[0], next_other_ref[0])


def finish_kernel(dp_ref, own_ref, next_ref, far_ref, mine_ref):
    half = far_ref.shape[0]
    core = lax.rem(dp_ref[0], 2)
    for i, extra in ((1 - core, ()), (core, (far_ref[...],))):
        rows = pl.ds(pl.multiple_of(half * i, half), half)
        mine_ref[rows] = add(own_ref[rows], next_ref[rows], *extra)


def refine_kernel(dp_ref, mine_ref, other_ref, fifth_ref, base_ref, gram_ref, refined_ref):
    summed = add(mine_ref[...], other_ref[...])

    def update(contract):
        gram = lax.dot_general(summed, summed, (((contract,), (contract,)), ((), ())), preferred_element_type=jnp.float32)
        gram_ref[...] = gram
        coupled = dot(fifth_ref[...], gram.astype(jnp.bfloat16))
        refined_ref[...] = (base_ref[...] - 0.25 * (1.0 - keep_rate) * coupled).astype(jnp.bfloat16)

    @pl.when(lax.rem(dp_ref[0], 2) == 0)
    def _():
        update(1)

    @pl.when(lax.rem(dp_ref[0], 2) != 0)
    def _():
        update(0)


def factor_kernel(factor_ref, gram_ref, fresh_ref):
    fresh_ref[...] = keep_rate * factor_ref[...] + (1.0 - keep_rate) * gram_ref[...]


def cost(flops, moved):
    return pl.CostEstimate(flops=flops, bytes_accessed=moved, transcendentals=0)


def local(grad_parts, factors, root_prev, plan):
    workers = lax.axis_size("mp")
    replicas = lax.axis_size("dp")
    size = factors.shape[-1]
    half = size // 2
    blocks = grad_parts[0, 0]
    ring = blocks.shape[0]
    dp = lax.axis_index("dp")

    def swapped(value):
        return lax.ppermute(value, "dp", [(i, i ^ 1) for i in range(replicas)])

    def around(value, step):
        pairs = [(i, (i // 2 + (1 - 2 * (i % 2)) * step) % ring * 2 + i % 2) for i in range(replicas)]
        return lax.ppermute(value, "dp", pairs)

    theirs = swapped(blocks)
    old_pieces = root_prev.reshape(workers, size // workers, size)
    initial = lax.all_to_all(old_pieces, "mp", split_axis=0, concat_axis=0, tiled=True).reshape(size, size)

    matrix = jax.ShapeDtypeStruct((size, size), jnp.bfloat16)
    part = jax.ShapeDtypeStruct((half, size), jnp.bfloat16)
    held = pltpu.with_memory_space_constraint(blocks, pltpu.HBM)
    place = dp.reshape(1)
    full = pl.BlockSpec((size, size), lambda i, place: (0, 0))
    one = pl.BlockSpec((half, size), lambda i, place: (0, 0))

    def next_chip(i, place):
        return lax.rem(lax.div(place[0], 2) + 1 + (ring - 2) * lax.rem(place[0], 2), ring), 0, 0

    ahead = pl.BlockSpec((1, size, size), next_chip)
    far = pl.BlockSpec(
        (1, half, size), lambda i, place: (lax.rem(lax.div(place[0], 2) + 2, ring), lax.rem(place[0], 2), 0)
    )

    def call(kernel, out_shape, in_specs, out_specs, *operands):
        return pl.pallas_call(
            kernel,
            out_shape=out_shape,
            grid_spec=pltpu.PrefetchScalarGridSpec(
                num_scalar_prefetch=1, grid=(1,), in_specs=in_specs, out_specs=out_specs
            ),
            compiler_params=PARAMS,
            cost_estimate=cost(0, 1),
        )(place, *operands)

    specs = [ahead, ahead, far, far]
    to_next, to_far = call(chip_kernel, (matrix, part), specs, (full, one), held, theirs, held, theirs)
    received = [around(to_far, 2), around(to_next, 1)]
    flops = 2 * size**3
    old_factor = pltpu.with_memory_space_constraint(factors[0, 0], pltpu.HBM)
    whole = jax.ShapeDtypeStruct((size, size), jnp.float32)
    fifth, base, own = pl.pallas_call(
        base_kernel,
        out_shape=(matrix, whole, matrix),
        in_specs=[SMEM, VMEM, HBM, HBM],
        out_specs=(VMEM, VMEM, VMEM),
        scratch_shapes=[pltpu.VMEM((size, size), jnp.float32), pltpu.SemaphoreType.DMA((2,))],
        compiler_params=PARAMS,
        cost_estimate=cost(9 * flops, 12 * size**2),
    )(place, initial, old_factor, held)
    fifth, base, own, *received = lax.optimization_barrier((fifth, base, own, *received))
    mine = call(finish_kernel, matrix, [full, full, one], full, own, received[1], received[0])
    other = swapped(mine)

    gram, refined = pl.pallas_call(
        refine_kernel,
        out_shape=(whole, matrix),
        in_specs=[SMEM] + [VMEM] * 4,
        out_specs=(VMEM, VMEM),
        compiler_params=PARAMS,
        cost_estimate=cost(2 * flops, 16 * size**2),
    )(place, mine, other, fifth, base)
    fresh_roots = lax.all_to_all(refined.reshape(old_pieces.shape), "mp", split_axis=0, concat_axis=0, tiled=True)
    fresh = pl.pallas_call(
        factor_kernel,
        out_shape=whole,
        in_specs=[VMEM, VMEM],
        out_specs=VMEM,
        compiler_params=PARAMS,
        cost_estimate=cost(0, 12 * size**2),
    )(factors[0, 0], gram)
    refresh = plan[0] < workers
    new_roots = jnp.where(refresh[:, None, None], fresh_roots, old_pieces).reshape(root_prev.shape)
    return fresh[None, None], new_roots


def solution(mesh):
    return jax.shard_map(
        local,
        mesh=mesh,
        in_specs=(
            P("dp", "mp", None, None, None),
            P("mp", "dp", None, None),
            P(None, "dp", "mp", None),
            P("dp", None),
        ),
        out_specs=(P("mp", "dp", None, None), P(None, "dp", "mp", None)),
        check_vma=False,
    )
```

```python
import jax
import jax.numpy as jnp
from jax import lax
from jax.experimental import pallas as pl
from jax.experimental.pallas import tpu as pltpu
from jax.sharding import PartitionSpec as P

keep_rate = 0.8
VMEM = pl.BlockSpec(memory_space=pltpu.VMEM)
HBM = pl.BlockSpec(memory_space=pltpu.HBM)
SMEM = pl.BlockSpec(memory_space=pltpu.SMEM)
PARAMS = pltpu.CompilerParams(vmem_limit_bytes=20 * 1024 * 1024)


def dot(a, b):
    return jnp.dot(a, b, preferred_element_type=jnp.float32)


def split(value):
    high = value.astype(jnp.bfloat16)
    return high, (value - high.astype(jnp.float32)).astype(jnp.bfloat16)


def fifth_kernel(dp_ref, root_ref, blocks_ref, high_ref, low_ref, own_ref, sem):
    load = pltpu.make_async_copy(blocks_ref.at[lax.div(dp_ref[0], 2)], own_ref, sem)
    load.start()
    root = root_ref[...]
    high, low = split(dot(root, root))
    high, low = split(dot(high, high) + (dot(high, low) + dot(low, high)))
    high_ref[...], low_ref[...] = split(dot(root, high) + dot(root, low))
    load.wait()


def base_kernel(root_ref, factor_ref, high_ref, low_ref, base_ref):
    factor, rest = split(factor_ref[...])
    coupled = dot(high_ref[...], factor) + (dot(high_ref[...], rest) + dot(low_ref[...], factor))
    base_ref[...] = 1.25 * root_ref[...].astype(jnp.float32) - 0.25 * keep_rate * coupled


def add(*values):
    return sum(value.astype(jnp.float32) for value in values).astype(jnp.bfloat16)


def chip_kernel(dp_ref, next_ref, next_other_ref, far_ref, far_other_ref, next_out_ref, far_out_ref):
    far_out_ref[...] = add(far_ref[0], far_other_ref[0])
    next_out_ref[...] = add(next_ref[0], next_other_ref[0])


def finish_kernel(dp_ref, own_ref, next_ref, far_ref, mine_ref):
    half = far_ref.shape[0]
    core = lax.rem(dp_ref[0], 2)
    for i, extra in ((1 - core, ()), (core, (far_ref[...],))):
        rows = pl.ds(pl.multiple_of(half * i, half), half)
        mine_ref[rows] = add(own_ref[rows], next_ref[rows], *extra)


def refine_kernel(dp_ref, mine_ref, other_ref, fifth_ref, base_ref, gram_ref, refined_ref):
    summed = add(mine_ref[...], other_ref[...])

    def update(contract):
        gram = lax.dot_general(summed, summed, (((contract,), (contract,)), ((), ())), preferred_element_type=jnp.float32)
        gram_ref[...] = gram
        coupled = dot(fifth_ref[...], gram.astype(jnp.bfloat16))
        refined_ref[...] = (base_ref[...] - 0.25 * (1.0 - keep_rate) * coupled).astype(jnp.bfloat16)

    @pl.when(lax.rem(dp_ref[0], 2) == 0)
    def _():
        update(1)

    @pl.when(lax.rem(dp_ref[0], 2) != 0)
    def _():
        update(0)


def factor_kernel(factor_ref, gram_ref, fresh_ref):
    fresh_ref[...] = keep_rate * factor_ref[...] + (1.0 - keep_rate) * gram_ref[...]


def cost(flops, moved):
    return pl.CostEstimate(flops=flops, bytes_accessed=moved, transcendentals=0)


def local(grad_parts, factors, root_prev, plan):
    workers = lax.axis_size("mp")
    replicas = lax.axis_size("dp")
    size = factors.shape[-1]
    half = size // 2
    blocks = grad_parts[0, 0]
    ring = blocks.shape[0]
    dp = lax.axis_index("dp")

    def swapped(value):
        return lax.ppermute(value, "dp", [(i, i ^ 1) for i in range(replicas)])

    def around(value, step):
        pairs = [(i, (i // 2 + (1 - 2 * (i % 2)) * step) % ring * 2 + i % 2) for i in range(replicas)]
        return lax.ppermute(value, "dp", pairs)

    theirs = swapped(blocks)
    old_pieces = root_prev.reshape(workers, size // workers, size)
    initial = lax.all_to_all(old_pieces, "mp", split_axis=0, concat_axis=0, tiled=True).reshape(size, size)

    matrix = jax.ShapeDtypeStruct((size, size), jnp.bfloat16)
    part = jax.ShapeDtypeStruct((half, size), jnp.bfloat16)
    held = pltpu.with_memory_space_constraint(blocks, pltpu.HBM)
    place = dp.reshape(1)
    full = pl.BlockSpec((size, size), lambda i, place: (0, 0))
    one = pl.BlockSpec((half, size), lambda i, place: (0, 0))

    def next_chip(i, place):
        return lax.rem(lax.div(place[0], 2) + 1 + (ring - 2) * lax.rem(place[0], 2), ring), 0, 0

    ahead = pl.BlockSpec((1, size, size), next_chip)
    far = pl.BlockSpec(
        (1, half, size), lambda i, place: (lax.rem(lax.div(place[0], 2) + 2, ring), lax.rem(place[0], 2), 0)
    )

    def call(kernel, out_shape, in_specs, out_specs, *operands):
        return pl.pallas_call(
            kernel,
            out_shape=out_shape,
            grid_spec=pltpu.PrefetchScalarGridSpec(
                num_scalar_prefetch=1, grid=(1,), in_specs=in_specs, out_specs=out_specs
            ),
            compiler_params=PARAMS,
            cost_estimate=cost(0, 1),
        )(place, *operands)

    specs = [ahead, ahead, far, far]
    to_next, to_far = call(chip_kernel, (matrix, part), specs, (full, one), held, theirs, held, theirs)
    received = [around(to_far, 2), around(to_next, 1)]
    flops = 2 * size**3
    whole = jax.ShapeDtypeStruct((size, size), jnp.float32)
    fifth, rest, own = pl.pallas_call(
        fifth_kernel,
        out_shape=(matrix, matrix, matrix),
        in_specs=[SMEM, VMEM, HBM],
        out_specs=(VMEM, VMEM, VMEM),
        scratch_shapes=[pltpu.SemaphoreType.DMA],
        compiler_params=PARAMS,
        cost_estimate=cost(6 * flops, 8 * size**2),
    )(place, initial, held)
    fifth, rest, own, *received = lax.optimization_barrier((fifth, rest, own, *received))
    mine = call(finish_kernel, matrix, [full, full, one], full, own, received[1], received[0])
    other = swapped(mine)
    base = pl.pallas_call(
        base_kernel,
        out_shape=whole,
        in_specs=[VMEM] * 4,
        out_specs=VMEM,
        compiler_params=PARAMS,
        cost_estimate=cost(3 * flops, 12 * size**2),
    )(initial, factors[0, 0], fifth, rest)

    gram, refined = pl.pallas_call(
        refine_kernel,
        out_shape=(whole, matrix),
        in_specs=[SMEM] + [VMEM] * 4,
        out_specs=(VMEM, VMEM),
        compiler_params=PARAMS,
        cost_estimate=cost(2 * flops, 16 * size**2),
    )(place, mine, other, fifth, base)
    fresh_roots = lax.all_to_all(refined.reshape(old_pieces.shape), "mp", split_axis=0, concat_axis=0, tiled=True)
    fresh = pl.pallas_call(
        factor_kernel,
        out_shape=whole,
        in_specs=[VMEM, VMEM],
        out_specs=VMEM,
        compiler_params=PARAMS,
        cost_estimate=cost(0, 12 * size**2),
    )(factors[0, 0], gram)
    refresh = plan[0] < workers
    new_roots = jnp.where(refresh[:, None, None], fresh_roots, old_pieces).reshape(root_prev.shape)
    return fresh[None, None], new_roots


def solution(mesh):
    return jax.shard_map(
        local,
        mesh=mesh,
        in_specs=(
            P("dp", "mp", None, None, None),
            P("mp", "dp", None, None),
            P(None, "dp", "mp", None),
            P("dp", None),
        ),
        out_specs=(P("mp", "dp", None, None), P(None, "dp", "mp", None)),
        check_vma=False,
    )
```

```python
import functools
import random

import jax
import jax.numpy as jnp
from jax import lax
from jax.experimental import pallas as pl
from jax.experimental.pallas import tpu as pltpu
from jax.sharding import PartitionSpec as P

keep_rate = 0.8
VMEM = pl.BlockSpec(memory_space=pltpu.VMEM)
HBM = pl.BlockSpec(memory_space=pltpu.HBM)
SMEM = pl.BlockSpec(memory_space=pltpu.SMEM)
PARAMS = pltpu.CompilerParams(vmem_limit_bytes=20 * 1024 * 1024)


def sending_order(workers):
    order = list(range(workers))
    random.Random(4).shuffle(order)
    return order


def dot(a, b):
    return jnp.dot(a, b, preferred_element_type=jnp.float32)


def split(value):
    high = value.astype(jnp.bfloat16)
    return high, (value - high.astype(jnp.float32)).astype(jnp.bfloat16)


def fifth_kernel(dp_ref, root_ref, blocks_ref, high_ref, low_ref, own_ref, sem):
    load = pltpu.make_async_copy(blocks_ref.at[lax.div(dp_ref[0], 2)], own_ref, sem)
    load.start()
    root = root_ref[...]
    high, low = split(dot(root, root))
    high, low = split(dot(high, high) + (dot(high, low) + dot(low, high)))
    high_ref[...], low_ref[...] = split(dot(root, high) + dot(root, low))
    load.wait()


def base_kernel(root_ref, factor_ref, high_ref, low_ref, base_ref):
    factor, rest = split(factor_ref[...])
    coupled = dot(high_ref[...], factor) + (dot(high_ref[...], rest) + dot(low_ref[...], factor))
    base_ref[...] = 1.25 * root_ref[...].astype(jnp.float32) - 0.25 * keep_rate * coupled


def add(*values):
    return sum(value.astype(jnp.float32) for value in values).astype(jnp.bfloat16)


def chip_kernel(dp_ref, next_ref, next_other_ref, far_ref, far_other_ref, next_out_ref, far_out_ref):
    far_out_ref[...] = add(far_ref[0], far_other_ref[0])
    next_out_ref[...] = add(next_ref[0], next_other_ref[0])


def finish_kernel(dp_ref, own_ref, next_ref, far_ref, mine_ref):
    half = far_ref.shape[0]
    core = lax.rem(dp_ref[0], 2)
    for i, extra in ((1 - core, ()), (core, (far_ref[...],))):
        rows = pl.ds(pl.multiple_of(half * i, half), half)
        mine_ref[rows] = add(own_ref[rows], next_ref[rows], *extra)


def refine_kernel(order, dp_ref, mine_ref, other_ref, fifth_ref, base_ref, gram_ref, refined_ref):
    summed = add(mine_ref[...], other_ref[...])

    def update(contract):
        gram = lax.dot_general(summed, summed, (((contract,), (contract,)), ((), ())), preferred_element_type=jnp.float32)
        gram_ref[...] = gram
        coupled = dot(fifth_ref[...], gram.astype(jnp.bfloat16))
        refined = base_ref[...] - 0.25 * (1.0 - keep_rate) * coupled
        rows = refined_ref.shape[1]
        for at, worker in enumerate(order):
            refined_ref[at] = refined[worker * rows : (worker + 1) * rows].astype(jnp.bfloat16)

    @pl.when(lax.rem(dp_ref[0], 2) == 0)
    def _():
        update(1)

    @pl.when(lax.rem(dp_ref[0], 2) != 0)
    def _():
        update(0)


def factor_kernel(factor_ref, gram_ref, fresh_ref):
    fresh_ref[...] = keep_rate * factor_ref[...] + (1.0 - keep_rate) * gram_ref[...]


def select_kernel(order, plan_ref, fresh_ref, old_ref, out_ref):
    for at, worker in enumerate(order):
        refresh = plan_ref[worker] < len(order)
        out_ref[worker] = jnp.where(refresh, fresh_ref[at], old_ref[worker])


def cost(flops, moved):
    return pl.CostEstimate(flops=flops, bytes_accessed=moved, transcendentals=0)


def local(grad_parts, factors, root_prev, plan):
    workers = lax.axis_size("mp")
    replicas = lax.axis_size("dp")
    size = factors.shape[-1]
    half = size // 2
    blocks = grad_parts[0, 0]
    ring = blocks.shape[0]
    dp = lax.axis_index("dp")

    def swapped(value):
        return lax.ppermute(value, "dp", [(i, i ^ 1) for i in range(replicas)])

    def around(value, step):
        pairs = [(i, (i // 2 + (1 - 2 * (i % 2)) * step) % ring * 2 + i % 2) for i in range(replicas)]
        return lax.ppermute(value, "dp", pairs)

    theirs = swapped(blocks)
    old_pieces = root_prev.reshape(workers, size // workers, size)
    initial = lax.all_to_all(old_pieces, "mp", split_axis=0, concat_axis=0, tiled=True).reshape(size, size)

    matrix = jax.ShapeDtypeStruct((size, size), jnp.bfloat16)
    part = jax.ShapeDtypeStruct((half, size), jnp.bfloat16)
    held = pltpu.with_memory_space_constraint(blocks, pltpu.HBM)
    place = dp.reshape(1)
    full = pl.BlockSpec((size, size), lambda i, place: (0, 0))
    one = pl.BlockSpec((half, size), lambda i, place: (0, 0))

    def next_chip(i, place):
        return lax.rem(lax.div(place[0], 2) + 1 + (ring - 2) * lax.rem(place[0], 2), ring), 0, 0

    ahead = pl.BlockSpec((1, size, size), next_chip)
    far = pl.BlockSpec(
        (1, half, size), lambda i, place: (lax.rem(lax.div(place[0], 2) + 2, ring), lax.rem(place[0], 2), 0)
    )

    def call(kernel, out_shape, in_specs, out_specs, *operands):
        return pl.pallas_call(
            kernel,
            out_shape=out_shape,
            grid_spec=pltpu.PrefetchScalarGridSpec(
                num_scalar_prefetch=1, grid=(1,), in_specs=in_specs, out_specs=out_specs
            ),
            compiler_params=PARAMS,
            cost_estimate=cost(0, 1),
        )(place, *operands)

    specs = [ahead, ahead, far, far]
    to_next, to_far = call(chip_kernel, (matrix, part), specs, (full, one), held, theirs, held, theirs)
    received = [around(to_far, 2), around(to_next, 1)]
    flops = 2 * size**3
    whole = jax.ShapeDtypeStruct((size, size), jnp.float32)
    fifth, rest, own = pl.pallas_call(
        fifth_kernel,
        out_shape=(matrix, matrix, matrix),
        in_specs=[SMEM, VMEM, HBM],
        out_specs=(VMEM, VMEM, VMEM),
        scratch_shapes=[pltpu.SemaphoreType.DMA],
        compiler_params=PARAMS,
        cost_estimate=cost(6 * flops, 8 * size**2),
    )(place, initial, held)
    fifth, rest, own, *received = lax.optimization_barrier((fifth, rest, own, *received))
    mine = call(finish_kernel, matrix, [full, full, one], full, own, received[1], received[0])
    other = swapped(mine)
    base = pl.pallas_call(
        base_kernel,
        out_shape=whole,
        in_specs=[VMEM] * 4,
        out_specs=VMEM,
        compiler_params=PARAMS,
        cost_estimate=cost(3 * flops, 12 * size**2),
    )(initial, factors[0, 0], fifth, rest)

    order = sending_order(workers)
    gram, refined = pl.pallas_call(
        functools.partial(refine_kernel, order),
        out_shape=(whole, jax.ShapeDtypeStruct(old_pieces.shape, jnp.bfloat16)),
        in_specs=[SMEM] + [VMEM] * 4,
        out_specs=(VMEM, VMEM),
        compiler_params=PARAMS,
        cost_estimate=cost(2 * flops, 16 * size**2),
    )(place, mine, other, fifth, base)
    fresh_roots = lax.all_to_all(
        refined, "mp", split_axis=0, concat_axis=0, tiled=True, axis_index_groups=[order]
    )
    fresh = pl.pallas_call(
        factor_kernel,
        out_shape=whole,
        in_specs=[VMEM, VMEM],
        out_specs=VMEM,
        compiler_params=PARAMS,
        cost_estimate=cost(0, 12 * size**2),
    )(factors[0, 0], gram)
    new_roots = pl.pallas_call(
        functools.partial(select_kernel, order),
        out_shape=jax.ShapeDtypeStruct(old_pieces.shape, jnp.bfloat16),
        in_specs=[SMEM, VMEM, VMEM],
        out_specs=VMEM,
        compiler_params=PARAMS,
        cost_estimate=cost(0, 6 * size**2),
    )(plan[0], fresh_roots, old_pieces)
    return fresh[None, None], new_roots.reshape(root_prev.shape)


def solution(mesh):
    return jax.shard_map(
        local,
        mesh=mesh,
        in_specs=(
            P("dp", "mp", None, None, None),
            P("mp", "dp", None, None),
            P(None, "dp", "mp", None),
            P("dp", None),
        ),
        out_specs=(P("mp", "dp", None, None), P(None, "dp", "mp", None)),
        check_vma=False,
    )
```

```python
import functools
import random

import jax
import jax.numpy as jnp
from jax import lax
from jax.experimental import pallas as pl
from jax.experimental.pallas import tpu as pltpu
from jax.sharding import PartitionSpec as P

keep_rate = 0.8
VMEM = pl.BlockSpec(memory_space=pltpu.VMEM)
HBM = pl.BlockSpec(memory_space=pltpu.HBM)
SMEM = pl.BlockSpec(memory_space=pltpu.SMEM)
PARAMS = pltpu.CompilerParams(vmem_limit_bytes=20 * 1024 * 1024)


def sending_order(workers):
    order = list(range(workers))
    random.Random(4).shuffle(order)
    return order


def dot(a, b):
    return jnp.dot(a, b, preferred_element_type=jnp.float32)


def split(value):
    high = value.astype(jnp.bfloat16)
    return high, (value - high.astype(jnp.float32)).astype(jnp.bfloat16)


def fifth_kernel(dp_ref, root_ref, blocks_ref, high_ref, low_ref, own_ref, sem):
    load = pltpu.make_async_copy(blocks_ref.at[lax.div(dp_ref[0], 2)], own_ref, sem)
    load.start()
    root = root_ref[...]
    high, low = split(dot(root, root))
    high, low = split(dot(high, high) + (dot(high, low) + dot(low, high)))
    high_ref[...], low_ref[...] = split(dot(root, high) + dot(root, low))
    load.wait()


def base_kernel(root_ref, factor_ref, high_ref, low_ref, base_ref):
    factor, rest = split(factor_ref[...])
    coupled = dot(high_ref[...], factor) + (dot(high_ref[...], rest) + dot(low_ref[...], factor))
    base_ref[...] = 1.25 * root_ref[...].astype(jnp.float32) - 0.25 * keep_rate * coupled


def add(*values):
    return sum(value.astype(jnp.float32) for value in values).astype(jnp.bfloat16)


def chip_kernel(dp_ref, next_ref, next_other_ref, far_ref, far_other_ref, next_out_ref, far_out_ref):
    far_out_ref[...] = add(far_ref[0], far_other_ref[0])
    next_out_ref[...] = add(next_ref[0], next_other_ref[0])


def finish_kernel(dp_ref, own_ref, next_ref, far_ref, mine_ref):
    half = far_ref.shape[0]
    core = lax.rem(dp_ref[0], 2)
    for i, extra in ((1 - core, ()), (core, (far_ref[...],))):
        rows = pl.ds(pl.multiple_of(half * i, half), half)
        mine_ref[rows] = add(own_ref[rows], next_ref[rows], *extra)


def refine_kernel(order, dp_ref, mine_ref, other_ref, fifth_ref, base_ref, gram_ref, out_ref, refined_ref, sem):
    summed = add(mine_ref[...], other_ref[...])

    def update(contract):
        gram = lax.dot_general(summed, summed, (((contract,), (contract,)), ((), ())), preferred_element_type=jnp.float32)
        gram_ref[...] = gram
        coupled = dot(fifth_ref[...], gram.astype(jnp.bfloat16))
        refined = base_ref[...] - 0.25 * (1.0 - keep_rate) * coupled
        rows = refined_ref.shape[1]
        for at, worker in enumerate(order):
            refined_ref[at] = refined[worker * rows : (worker + 1) * rows].astype(jnp.bfloat16)
        copy = pltpu.make_async_copy(refined_ref, out_ref, sem)
        copy.start()
        copy.wait()

    @pl.when(lax.rem(dp_ref[0], 2) == 0)
    def _():
        update(1)

    @pl.when(lax.rem(dp_ref[0], 2) != 0)
    def _():
        update(0)


def factor_kernel(factor_ref, gram_ref, fresh_ref):
    fresh_ref[...] = keep_rate * factor_ref[...] + (1.0 - keep_rate) * gram_ref[...]


def select_kernel(order, plan_ref, fresh_ref, old_ref, out_ref):
    for at, worker in enumerate(order):
        refresh = plan_ref[worker] < len(order)
        out_ref[worker] = jnp.where(refresh, fresh_ref[at], old_ref[worker])


def cost(flops, moved):
    return pl.CostEstimate(flops=flops, bytes_accessed=moved, transcendentals=0)


def local(grad_parts, factors, root_prev, plan):
    workers = lax.axis_size("mp")
    replicas = lax.axis_size("dp")
    size = factors.shape[-1]
    half = size // 2
    blocks = grad_parts[0, 0]
    ring = blocks.shape[0]
    dp = lax.axis_index("dp")

    def swapped(value):
        return lax.ppermute(value, "dp", [(i, i ^ 1) for i in range(replicas)])

    def around(value, step):
        pairs = [(i, (i // 2 + (1 - 2 * (i % 2)) * step) % ring * 2 + i % 2) for i in range(replicas)]
        return lax.ppermute(value, "dp", pairs)

    theirs = swapped(blocks)
    old_pieces = root_prev.reshape(workers, size // workers, size)
    initial = lax.all_to_all(old_pieces, "mp", split_axis=0, concat_axis=0, tiled=True).reshape(size, size)

    matrix = jax.ShapeDtypeStruct((size, size), jnp.bfloat16)
    part = jax.ShapeDtypeStruct((half, size), jnp.bfloat16)
    held = pltpu.with_memory_space_constraint(blocks, pltpu.HBM)
    place = dp.reshape(1)
    full = pl.BlockSpec((size, size), lambda i, place: (0, 0))
    one = pl.BlockSpec((half, size), lambda i, place: (0, 0))

    def next_chip(i, place):
        return lax.rem(lax.div(place[0], 2) + 1 + (ring - 2) * lax.rem(place[0], 2), ring), 0, 0

    ahead = pl.BlockSpec((1, size, size), next_chip)
    far = pl.BlockSpec(
        (1, half, size), lambda i, place: (lax.rem(lax.div(place[0], 2) + 2, ring), lax.rem(place[0], 2), 0)
    )

    def call(kernel, out_shape, in_specs, out_specs, *operands):
        return pl.pallas_call(
            kernel,
            out_shape=out_shape,
            grid_spec=pltpu.PrefetchScalarGridSpec(
                num_scalar_prefetch=1, grid=(1,), in_specs=in_specs, out_specs=out_specs
            ),
            compiler_params=PARAMS,
            cost_estimate=cost(0, 1),
        )(place, *operands)

    specs = [ahead, ahead, far, far]
    to_next, to_far = call(chip_kernel, (matrix, part), specs, (full, one), held, theirs, held, theirs)
    received = [around(to_far, 2), around(to_next, 1)]
    flops = 2 * size**3
    whole = jax.ShapeDtypeStruct((size, size), jnp.float32)
    fifth, rest, own = pl.pallas_call(
        fifth_kernel,
        out_shape=(matrix, matrix, matrix),
        in_specs=[SMEM, VMEM, HBM],
        out_specs=(VMEM, VMEM, VMEM),
        scratch_shapes=[pltpu.SemaphoreType.DMA],
        compiler_params=PARAMS,
        cost_estimate=cost(6 * flops, 8 * size**2),
    )(place, initial, held)
    fifth, rest, own, *received = lax.optimization_barrier((fifth, rest, own, *received))
    mine = call(finish_kernel, matrix, [full, full, one], full, own, received[1], received[0])
    other = swapped(mine)
    base = pl.pallas_call(
        base_kernel,
        out_shape=whole,
        in_specs=[VMEM] * 4,
        out_specs=VMEM,
        compiler_params=PARAMS,
        cost_estimate=cost(3 * flops, 12 * size**2),
    )(initial, factors[0, 0], fifth, rest)

    order = sending_order(workers)
    gram, refined = pl.pallas_call(
        functools.partial(refine_kernel, order),
        out_shape=(whole, jax.ShapeDtypeStruct(old_pieces.shape, jnp.bfloat16)),
        in_specs=[SMEM] + [VMEM] * 4,
        out_specs=(VMEM, HBM),
        scratch_shapes=[pltpu.VMEM(old_pieces.shape, jnp.bfloat16), pltpu.SemaphoreType.DMA],
        compiler_params=PARAMS,
        cost_estimate=cost(2 * flops, 16 * size**2),
    )(place, mine, other, fifth, base)
    fresh_roots = lax.all_to_all(
        refined, "mp", split_axis=0, concat_axis=0, tiled=True, axis_index_groups=[order]
    )
    fresh = pl.pallas_call(
        factor_kernel,
        out_shape=whole,
        in_specs=[VMEM, VMEM],
        out_specs=VMEM,
        compiler_params=PARAMS,
        cost_estimate=cost(0, 12 * size**2),
    )(factors[0, 0], gram)
    new_roots = pl.pallas_call(
        functools.partial(select_kernel, order),
        out_shape=jax.ShapeDtypeStruct(old_pieces.shape, jnp.bfloat16),
        in_specs=[SMEM, VMEM, VMEM],
        out_specs=VMEM,
        compiler_params=PARAMS,
        cost_estimate=cost(0, 6 * size**2),
    )(plan[0], fresh_roots, old_pieces)
    return fresh[None, None], new_roots.reshape(root_prev.shape)


def solution(mesh):
    return jax.shard_map(
        local,
        mesh=mesh,
        in_specs=(
            P("dp", "mp", None, None, None),
            P("mp", "dp", None, None),
            P(None, "dp", "mp", None),
            P("dp", None),
        ),
        out_specs=(P("mp", "dp", None, None), P(None, "dp", "mp", None)),
        check_vma=False,
    )
```
